256 devices in a mesh: gx: 16 (over x, y_lo, core), gy: 16 (over y_hi, z).
Axes of the slice: x: 4, y: 4 (y_hi: 2, y_lo: 2; y = y_hi * 2 + y_lo), z: 8, core: 2. Of those that a mesh axis runs over, the one named last changes fastest.
Arguments:
- tokens: bfloat16 [1024, 8192], P('gx'), may hold values from -6 to 6
- gate_weight: bfloat16 [8192, 28672], P('gx', 'gy'), may hold values from -0.0625 to 0.0625
- up_weight: bfloat16 [8192, 28672], P('gx', 'gy'), may hold values from -0.0625 to 0.0625
- down_weight: bfloat16 [28672, 8192], P('gy', 'gx'), may hold values from -0.03125 to 0.03125
- valid_counts: int32 [16], replicated, may hold values from 1 to 64, 768 in all
Outputs:
- mixed: float32 [1024, 8192], P('gy', 'gx')
The draws below stay inside these ranges and needn't reach their ends.
Inputs may be any that keep to these rules, and one draw needn't show every extreme that they name: valid_counts sum to 768 and the largest equals 64.
All inputs are finite; a program needn't handle non-finite values.
Results may differ from the reference program's by a relative error of at most 0.0029.
Values may be sent and summed in bfloat16 or wider, within the bound.
A program may use at most 128 MiB of HBM per device.

```python
import math
import jax
import jax.numpy as jnp
import numpy as np

D = 8192
FF = 28672
ROWS = 64
TOKENS = 1024
N_GX = 16


def shard_levels(stream_key, dims, pieces, least, high):
    def one(position, shards_of):
        heights = jax.random.uniform(jax.random.fold_in(jax.random.fold_in(stream_key, 6), position), (shards_of,), jnp.float32, least / len(pieces), high / len(pieces))
        return jnp.repeat(jnp.exp(heights), dims[position] // shards_of).reshape((-1,) + (1,) * (len(dims) - position - 1))

    gain = one(*pieces[0])
    for cut in pieces[1:]:
        gain = gain * one(*cut)
    return gain


def length_profile(number_of, total, bound, skew):
    portions = [(1 << 20) // math.isqrt(rank ** skew) + 1 for rank in range(2, number_of + 1)]
    rest, given = total - bound - (number_of - 1), [1] * (number_of - 1)
    while rest > 0:
        movable = [i for i in range(number_of - 1) if given[i] < bound]
        mass, left = sum([portions[i] for i in movable]), rest
        for i in movable:
            addition = min(bound - given[i], max(1, left * portions[i] // mass), rest)
            given[i] = given[i] + addition
            rest = rest - addition
    return np.array([bound] + given)


def uneven(own_key, number_of, total, bound, skew):
    if number_of == 2:
        one = jax.random.randint(own_key, (), max(1, total - bound), min(bound, total - 1) + 1)
        return jnp.stack([one, total - one])
    sizes = jnp.asarray(length_profile(number_of, total, bound, skew), jnp.int32)
    twos = (number_of - 1) // 2
    donor, receiver = sizes[1:1 + 2 * twos:2], sizes[2:2 + 2 * twos:2]
    room = jnp.minimum(donor - 1, bound - receiver)
    passed = jax.random.randint(jax.random.fold_in(own_key, 1), (twos,), 0, 1 << 20) % (room + 1)
    sizes = sizes.at[1:1 + 2 * twos:2].set(donor - passed).at[2:2 + 2 * twos:2].set(receiver + passed)
    return sizes[jax.random.permutation(jax.random.fold_in(own_key, 2), number_of)]


def normal_values(rng, shape, deviation, limit, pieces=(), held_as=jnp.bfloat16):
    result = jax.random.normal(rng, shape, jnp.float32) * deviation
    if len(pieces) > 0:
        result = shard_levels(rng, shape, pieces, -0.22, 0.18) * result
    return jnp.clip(result, min=-limit, max=limit).astype(held_as)


def setup_inputs(seed: int = 0) -> dict:
    keys = jax.random.split(jax.random.key(seed), 6)
    return {
        "tokens": normal_values(keys[0], (TOKENS, D), 1.0, 6.0, ((0, 16),)),
        "gate_weight": normal_values(keys[1], (D, FF), D ** -0.5, 0.0625, ((0, 16), (1, 16))),
        "up_weight": normal_values(keys[2], (D, FF), D ** -0.5, 0.0625, ((0, 16), (1, 16))),
        "down_weight": normal_values(keys[3], (FF, D), FF ** -0.5, 0.03125, ((0, 16), (1, 16))),
        "valid_counts": uneven(keys[4], N_GX, N_GX * ROWS * 3 // 4, ROWS, 1).astype(jnp.int32),
    }


def reference(tokens, gate_weight, up_weight, down_weight, valid_counts):
    slot_index = jnp.arange(TOKENS, dtype=jnp.int32)
    group_of = slot_index // ROWS
    live_rows = ((slot_index % ROWS) < valid_counts[group_of]).astype(jnp.int32)
    gate_sum = jnp.dot(tokens, gate_weight, preferred_element_type=jnp.float32)
    up_sum = jnp.dot(tokens, up_weight, preferred_element_type=jnp.float32)
    hidden = jnp.where(live_rows[:, None] == 1, jax.nn.silu(gate_sum) * up_sum, jnp.float32(0.0)).astype(jnp.bfloat16)
    return jnp.dot(hidden, down_weight, preferred_element_type=jnp.float32)
```

```python
import functools

import jax
import jax.numpy as jnp
from jax import lax
from jax.experimental import pallas as pl
from jax.experimental.pallas import tpu as pltpu
from jax.sharding import PartitionSpec as P

MESH = pl.DeviceIdType.MESH
BF16, F32, I16, I32 = jnp.bfloat16, jnp.float32, jnp.int16, jnp.int32

N = 16
CHIPS = 8
ROWS = 64
LIVE = 768
CHUNKS = 3
M = LIVE // CHUNKS
MC = M // CHIPS
MZ = M // N
SPAN = 8
WINDOW = 20
DEST = 5
FULL = 32000.0


def aligned(index, unit):
    return pl.ds(pl.multiple_of(index * unit, unit), unit)


def kernel(
    counts, tokens, gate, up, down, out,
    tok, wg, wu, wd, xs, qs, qr, hid, part, zs, zr, zsum, fin,
    local_sem, tok_send, tok_recv, w_send, w_recv, x_send, x_recv,
    q_send, q_recv, h_send, h_recv, f_send, f_recv, z_send, z_recv, e_send, e_recv, e_local,
):
    gx, gy = lax.axis_index("gx"), lax.axis_index("gy")
    chip, core = gx // 2, gx % 2
    depth = gate.shape[0]
    half = gate.shape[1] // 2
    width = down.shape[1]
    sibling = (gx + 1 - 2 * core, gy)

    def remote(src, dst, send, recv, device):
        return pltpu.make_async_remote_copy(
            src_ref=src, dst_ref=dst, send_sem=send, recv_sem=recv, device_id=device, device_id_type=MESH
        )

    def peer_chip(d):
        return (chip + d) % CHIPS

    mine = aligned(core, half)
    my_rows = aligned(core, depth)
    local = [
        pltpu.make_async_copy(tokens.at[:, aligned(gx, depth)], tok.at[aligned(gx, ROWS)], local_sem.at[0]),
        pltpu.make_async_copy(gate.at[:, mine], wg.at[my_rows], local_sem.at[1]),
        pltpu.make_async_copy(up.at[:, mine], wu.at[my_rows], local_sem.at[2]),
        pltpu.make_async_copy(down, wd, local_sem.at[3]),
    ]
    for copy in local:
        copy.start()
    fin[...] = jnp.zeros_like(fin)

    barrier = pltpu.get_barrier_semaphore()

    def greet(d, carry):
        pl.semaphore_signal(barrier, inc=1, device_id=((gx + d) % N, gy), device_id_type=MESH)
        pl.semaphore_signal(barrier, inc=1, device_id=(gx, (gy + d) % N), device_id_type=MESH)
        return carry

    lax.fori_loop(1, N, greet, 0)
    pl.semaphore_wait(barrier, 2 * (N - 1))

    def token_copy(d):
        to = (gx + d) % N
        return remote(
            tokens.at[:, aligned(to, depth)], tok.at[aligned(gx, ROWS)], tok_send.at[d], tok_recv.at[gx], (to, gy)
        )

    def start_tokens(d, carry):
        token_copy(d).start()
        return carry

    lax.fori_loop(1, N, start_tokens, 0)

    theirs = aligned(1 - core, half)
    weights = [
        remote(gate.at[:, theirs], wg.at[my_rows], w_send.at[0], w_recv.at[0], sibling),
        remote(up.at[:, theirs], wu.at[my_rows], w_send.at[1], w_recv.at[1], sibling),
    ]
    for copy in weights:
        copy.start()

    count = [counts[g] for g in range(N)]
    first = [jnp.int32(0)]
    for g in range(N - 1):
        first.append(first[-1] + count[g])

    def wait_tokens(g, carry):
        @pl.when(g != gx)
        def _():
            remote(tok.at[aligned(g, ROWS)], tok.at[aligned(g, ROWS)], tok_send.at[0], tok_recv.at[g], (g, gy)).wait_recv()

        return carry

    def compact(k):
        lane = lax.broadcasted_iota(I32, (1, SPAN * ROWS), 1)
        place = jnp.full((1, SPAN * ROWS), -1, I32)
        for i in range(SPAN):
            g = 4 * k + i
            slot = lane - ROWS * i
            place = jnp.where((slot >= 0) & (slot < count[g]), slot + (first[g] - M * k), place)
        row = lax.broadcasted_iota(I32, (M, SPAN * ROWS), 0)
        pick = jnp.where(row == place, 1.0, 0.0).astype(BF16)
        rows = jnp.dot(pick, tok[pl.ds(4 * k * ROWS, SPAN * ROWS), :], preferred_element_type=F32)
        xs[k, :, my_rows] = rows.astype(BF16)

    def x_copy(k):
        return remote(xs.at[k, :, my_rows], xs.at[k, :, my_rows], x_send.at[k], x_recv.at[k], sibling)

    local[0].wait()
    for k in range(CHUNKS):
        lax.fori_loop(0 if k == 0 else 4 * k + 4, 4 * k + 8, wait_tokens, 0)
        compact(k)
        x_copy(k).start()

    for copy in local[1:3]:
        copy.wait()
    for copy in weights:
        copy.wait_recv()

    def q_copy(k, d):
        to = peer_chip(d)
        return remote(
            qs.at[k, aligned(to, MC)], qr.at[k, chip], q_send.at[k, d], q_recv.at[k, chip], (2 * to + core, gy)
        )

    def project(k):
        x = xs[k]
        g = jnp.dot(x, wg[...], preferred_element_type=F32)
        u = jnp.dot(x, wu[...], preferred_element_type=F32)
        top = jnp.maximum(jnp.max(jnp.abs(g), axis=1, keepdims=True), jnp.max(jnp.abs(u), axis=1, keepdims=True))
        level = jnp.ceil(jnp.log(jnp.maximum(top, 1e-30)) * (64.0 / 0.6931471805599453)) + 1.0
        to_code = FULL * jnp.exp2(level * (-1.0 / 64.0))
        qs[k, :, :half] = jnp.round(g * to_code).astype(I32).astype(I16)
        qs[k, :, half : 2 * half] = jnp.round(u * to_code).astype(I32).astype(I16)
        qs[k, :, 2 * half :] = jnp.broadcast_to(level.astype(I32), (M, 128)).astype(I16)

    for k in range(CHUNKS):
        x_copy(k).wait_recv()
        project(k)

        def start_sums(d, carry, k=k):
            q_copy(k, d).start()
            return carry

        lax.fori_loop(1, CHIPS, start_sums, 0)

    def h_copy(k, d):
        to = peer_chip(d)
        block = hid.at[k, aligned(chip, MC), mine]
        return remote(block, block, h_send.at[k, d], h_recv.at[k, chip], (2 * to + core, gy))

    def decode(block):
        scale = jnp.exp2(block[:, 2 * half :].astype(I32).astype(F32)[:, :1] * (1.0 / 64.0)) * (1.0 / FULL)
        return block[:, : 2 * half].astype(I32).astype(F32) * scale

    def activate(k):
        total = decode(qs[k, aligned(chip, MC), :])
        for d in range(1, CHIPS):
            source = peer_chip(d)
            remote(qr.at[k, source], qr.at[k, source], q_send.at[k, 0], q_recv.at[k, source], sibling).wait_recv()
            total = total + decode(qr[k, source])
        g, u = total[:, :half], total[:, half:]
        hid[k, aligned(chip, MC), mine] = (g / (1.0 + jnp.exp(-g)) * u).astype(BF16)

        def start_hidden(d, carry):
            h_copy(k, d).start()
            return carry

        lax.fori_loop(1, CHIPS, start_hidden, 0)

    def f_copy(k):
        return remote(hid.at[k, :, mine], hid.at[k, :, mine], f_send.at[k], f_recv.at[k], sibling)

    def forward(k):
        def wait_hidden(d, carry):
            source = peer_chip(d)
            block = hid.at[k, aligned(source, MC), mine]
            remote(block, block, h_send.at[k, 0], h_recv.at[k, source], sibling).wait_recv()
            return carry

        lax.fori_loop(1, CHIPS, wait_hidden, 0)
        f_copy(k).start()

    def z_copy(k, d):
        to = (gy + d) % N
        return remote(zs.at[k, aligned(to, MZ)], zr.at[k, gy], z_send.at[k, d], z_recv.at[k, gy], (gx, to))

    def contract(k):
        f_copy(k).wait_recv()
        o = jnp.dot(hid[k], wd[...], preferred_element_type=F32)
        part[k] = o
        zs[k] = o.astype(BF16)

        def start_out(d, carry):
            z_copy(k, d).start()
            return carry

        lax.fori_loop(1, N, start_out, 0)

    def e_copy(k, i):
        to = 4 * k + gy // 4 + i
        place = (N * k + gy) - 4 * to + 16
        return to, place

    def collect(k):
        def add(d, total):
            source = (gy + d) % N
            remote(zr.at[k, source], zr.at[k, source], z_send.at[k, 0], z_recv.at[k, source], sibling).wait_recv()
            return total + zr[k, source].astype(F32)

        zsum[k] = lax.fori_loop(1, N, add, part[k, aligned(gy, MZ), :])
        for i in range(DEST):
            to, place = e_copy(k, i)

            @pl.when(to == gy)
            def _():
                pltpu.make_async_copy(zsum.at[k], fin.at[place], e_local.at[k]).start()

            @pl.when(to != gy)
            def _():
                remote(zsum.at[k], fin.at[place], e_send.at[k, i], e_recv.at[place], (gx, to)).start()

    activate(0)
    activate(1)
    forward(0)
    local[3].wait()
    activate(2)
    contract(0)
    forward(1)
    contract(1)
    forward(2)
    collect(0)
    contract(2)
    collect(1)
    collect(2)

    def wait_rows(place, carry):
        block = 4 * gy - 16 + place

        @pl.when((block >= 0) & (block < N * CHUNKS) & (block % N != gy))
        def _():
            remote(zsum.at[0], fin.at[place], e_send.at[0, 0], e_recv.at[place], sibling).wait_recv()

        return carry

    lax.fori_loop(0, WINDOW, wait_rows, 0)
    for k in range(CHUNKS):
        for i in range(DEST):
            to, place = e_copy(k, i)

            @pl.when(to == gy)
            def _():
                pltpu.make_async_copy(zsum.at[k], fin.at[place], e_local.at[k]).wait()

    my_count, my_first = jnp.int32(0), jnp.int32(0)
    for g in range(N):
        my_count = my_count + jnp.where(g == gy, count[g], 0)
        my_first = my_first + jnp.where(g < gy, count[g], 0)
    slot = lax.broadcasted_iota(I32, (ROWS, WINDOW * MZ), 0)
    live = lax.broadcasted_iota(I32, (ROWS, WINDOW * MZ), 1) + (ROWS * gy - 256) - my_first
    pick = jnp.where((live == slot) & (slot < my_count), 1.0, 0.0).astype(BF16)
    rest = fin[...].reshape(WINDOW * MZ, width)
    total = jnp.zeros((ROWS, width), F32)
    for _ in range(3):
        term = rest.astype(BF16)
        total = total + jnp.dot(pick, term, preferred_element_type=F32)
        rest = rest - term.astype(F32)
    out[...] = total

    for copy in weights:
        copy.wait_send()

    def sent_tokens(d, carry):
        token_copy(d).wait_send()
        return carry

    lax.fori_loop(1, N, sent_tokens, 0)
    for k in range(CHUNKS):
        x_copy(k).wait_send()
        f_copy(k).wait_send()

        def sent_chip(d, carry, k=k):
            q_copy(k, d).wait_send()
            h_copy(k, d).wait_send()
            return carry

        def sent_out(d, carry, k=k):
            z_copy(k, d).wait_send()
            return carry

        lax.fori_loop(1, CHIPS, sent_chip, 0)
        lax.fori_loop(1, N, sent_out, 0)
        for i in range(DEST):
            to, place = e_copy(k, i)

            @pl.when(to != gy)
            def _():
                remote(zsum.at[k], fin.at[place], e_send.at[k, i], e_recv.at[place], (gx, to)).wait_send()


def body(tokens, gate, up, down, counts):
    depth, hidden = gate.shape
    width = down.shape[1]
    half = hidden // 2
    code = 2 * half + 128
    dma = pltpu.SemaphoreType.DMA
    any_space = pl.BlockSpec(memory_space=pl.ANY)
    return pl.pallas_call(
        kernel,
        out_shape=jax.ShapeDtypeStruct((ROWS, width), F32),
        in_specs=[pl.BlockSpec(memory_space=pltpu.SMEM)] + [any_space] * 4,
        out_specs=pl.BlockSpec(memory_space=pltpu.VMEM),
        scratch_shapes=[
            pltpu.VMEM((N * ROWS, depth), BF16),
            pltpu.VMEM((2 * depth, half), BF16),
            pltpu.VMEM((2 * depth, half), BF16),
            pltpu.VMEM((hidden, width), BF16),
            pltpu.VMEM((CHUNKS, M, 2 * depth), BF16),
            pltpu.VMEM((CHUNKS, M, code), I16),
            pltpu.VMEM((CHUNKS, CHIPS, MC, code), I16),
            pltpu.VMEM((CHUNKS, M, hidden), BF16),
            pltpu.VMEM((CHUNKS, M, width), F32),
            pltpu.VMEM((CHUNKS, M, width), BF16),
            pltpu.VMEM((CHUNKS, N, MZ, width), BF16),
            pltpu.VMEM((CHUNKS, MZ, width), F32),
            pltpu.VMEM((WINDOW, MZ, width), F32),
            dma((4,)),
            dma((N,)), dma((N,)),
            dma((2,)), dma((2,)),
            dma((CHUNKS,)), dma((CHUNKS,)),
            dma((CHUNKS, CHIPS)), dma((CHUNKS, CHIPS)),
            dma((CHUNKS, CHIPS)), dma((CHUNKS, CHIPS)),
            dma((CHUNKS,)), dma((CHUNKS,)),
            dma((CHUNKS, N)), dma((CHUNKS, N)),
            dma((CHUNKS, DEST)), dma((WINDOW,)),
            dma((CHUNKS,)),
        ],
        compiler_params=pltpu.CompilerParams(
            collective_id=0, has_side_effects=True, vmem_limit_bytes=56 * 2**20
        ),
        name="swiglu",
    )(counts, tokens, gate, up, down)


def solution(mesh):
    in_specs = (P("gx", None), P("gx", "gy"), P("gx", "gy"), P("gy", "gx"), P())
    out_specs = P("gy", "gx")
    return jax.shard_map(body, mesh=mesh, in_specs=in_specs, out_specs=out_specs, check_vma=False)
```

```python
import functools

import jax
import jax.numpy as jnp
from jax import lax
from jax.experimental import pallas as pl
from jax.experimental.pallas import tpu as pltpu
from jax.sharding import PartitionSpec as P

MESH = pl.DeviceIdType.MESH
BF16, F32, I16, I32 = jnp.bfloat16, jnp.float32, jnp.int16, jnp.int32

N = 16
CHIPS = 8
NX = 4
ROWS = 64
LIVE = 768
TYPES = (0, 1, 0, 0, 1, 0)
CHUNKS = len(TYPES)
M = LIVE // CHUNKS
MC = M // CHIPS
MZ = 16
OWNERS = M // MZ
ORDER = (
    (0, 0), (0, 1), (0, 2), (0, 3), (0, 4), (0, 5), (1, 0), (1, 1), (1, 2), (1, 4), (2, 0), (1, 3),
    (2, 2), (3, 0), (1, 5), (2, 3), (2, 1), (3, 2), (2, 4), (4, 0), (2, 5), (3, 1), (3, 3), (5, 0),
    (4, 2), (3, 5), (3, 4), (5, 2), (4, 1), (4, 3), (5, 1), (5, 3), (6, 0), (4, 4), (4, 5), (5, 4),
    (6, 2), (5, 5), (6, 1), (6, 3), (6, 4), (6, 5),
)
SPAN = 6
WINDOW = 20
DEST = 5
FULL = 32000.0


def aligned(index, unit):
    return pl.ds(pl.multiple_of(index * unit, unit), unit)


def kernel(
    counts, tokens, gate, up, down, out,
    tok, wg, wu, wd, xs, qs, q1, qm, q2, hid, part, zs, zr, ecode, fin,
    local_sem, tok_send, tok_recv, w_send, w_recv, x_send, x_recv,
    a_send, a_recv, b_send, b_recv, h_send, h_recv, g_send, g_recv, f_send, f_recv,
    z_send, z_recv, e_send, e_recv, e_local,
):
    gx, gy = lax.axis_index("gx"), lax.axis_index("gy")
    along_x, along_y, core = gx // 4, gx // 2 % 2, gx % 2
    depth = gate.shape[0]
    half = gate.shape[1] // 2
    width = down.shape[1]
    sibling = (gx + 1 - 2 * core, gy)
    across = (gx + 2 - 4 * along_y, gy)

    def remote(src, dst, send, recv, device):
        return pltpu.make_async_remote_copy(
            src_ref=src, dst_ref=dst, send_sem=send, recv_sem=recv, device_id=device, device_id_type=MESH
        )

    def peer_x(d):
        to = (along_x + d) % NX
        return to, (4 * to + 2 * along_y + core, gy)

    mine = aligned(core, half)
    my_rows = aligned(core, depth)
    local = [
        pltpu.make_async_copy(tokens.at[:, aligned(gx, depth)], tok.at[aligned(gx, ROWS)], local_sem.at[0]),
        pltpu.make_async_copy(gate.at[:, mine], wg.at[my_rows], local_sem.at[1]),
        pltpu.make_async_copy(up.at[:, mine], wu.at[my_rows], local_sem.at[2]),
        pltpu.make_async_copy(down, wd, local_sem.at[3]),
    ]
    for copy in local:
        copy.start()
    fin[...] = jnp.zeros_like(fin)

    barrier = pltpu.get_barrier_semaphore()

    def greet(d, carry):
        pl.semaphore_signal(barrier, inc=1, device_id=((gx + d) % N, gy), device_id_type=MESH)
        pl.semaphore_signal(barrier, inc=1, device_id=(gx, (gy + d) % N), device_id_type=MESH)
        return carry

    with jax.named_scope("enter"):
        lax.fori_loop(1, N, greet, 0)
        pl.semaphore_wait(barrier, 2 * (N - 1))

    def token_copy(d):
        to = (gx + d) % N
        return remote(
            tokens.at[:, aligned(to, depth)], tok.at[aligned(gx, ROWS)], tok_send.at[d], tok_recv.at[gx], (to, gy)
        )

    def start_tokens(d, carry):
        token_copy(d).start()
        return carry

    lax.fori_loop(1, N, start_tokens, 0)

    theirs = aligned(1 - core, half)
    weights = [
        remote(gate.at[:, theirs], wg.at[my_rows], w_send.at[0], w_recv.at[0], sibling),
        remote(up.at[:, theirs], wu.at[my_rows], w_send.at[1], w_recv.at[1], sibling),
    ]
    for copy in weights:
        copy.start()

    count = [counts[g] for g in range(N)]
    first = [jnp.int32(0)]
    for g in range(N - 1):
        first.append(first[-1] + count[g])

    def wait_tokens(g, carry):
        @pl.when(g != gx)
        def _():
            remote(tok.at[aligned(g, ROWS)], tok.at[aligned(g, ROWS)], tok_send.at[0], tok_recv.at[g], (g, gy)).wait_recv()

        return carry

    def compact(k):
        lane = lax.broadcasted_iota(I32, (1, SPAN * ROWS), 1)
        place = jnp.full((1, SPAN * ROWS), -1, I32)
        for i in range(SPAN):
            g = 2 * k + i
            slot = lane - ROWS * i
            place = jnp.where((slot >= 0) & (slot < count[g]), slot + (first[g] - M * k), place)
        row = lax.broadcasted_iota(I32, (M, SPAN * ROWS), 0)
        pick = jnp.where(row == place, 1.0, 0.0).astype(BF16)
        rows = jnp.dot(pick, tok[pl.ds(2 * k * ROWS, SPAN * ROWS), :], preferred_element_type=F32)
        xs[k, :, my_rows] = rows.astype(BF16)

    def x_copy(k):
        return remote(xs.at[k, :, my_rows], xs.at[k, :, my_rows], x_send.at[k], x_recv.at[k], sibling)

    local[0].wait()
    for k in range(CHUNKS):
        with jax.named_scope(f"tokens{k}"):
            lax.fori_loop(0 if k == 0 else 2 * k + 4, 2 * k + 6, wait_tokens, 0)
        with jax.named_scope(f"compact{k}"):
            compact(k)
            x_copy(k).start()

    for copy in local[1:3]:
        copy.wait()
    for copy in weights:
        copy.wait_recv()

    def encode(ref, parts):
        top = functools.reduce(jnp.maximum, [jnp.max(jnp.abs(v), axis=1, keepdims=True) for v in parts])
        level = jnp.ceil(jnp.log(jnp.maximum(top, 1e-30)) * (64.0 / 0.6931471805599453)) + 1.0
        to_code = FULL * jnp.exp2(level * (-1.0 / 64.0))
        at = 0
        for v in parts:
            ref[:, at : at + v.shape[1]] = jnp.round(v * to_code).astype(I32).astype(I16)
            at += v.shape[1]
        ref[:, at:] = jnp.broadcast_to(level.astype(I32), (top.shape[0], 128)).astype(I16)

    def decode(ref):
        block = ref[...].astype(I32).astype(F32)
        used = block.shape[-1] - 128
        return block[..., :used] * (jnp.exp2(block[..., used : used + 1] * (1.0 / 64.0)) * (1.0 / FULL))

    def to_x(k, size, rows=None):
        copies = []
        for d in range(1, NX):
            to, device = peer_x(d)
            copies.append((aligned(to if rows is None else rows, size), aligned(along_x, size), d, along_x, device))
        return copies

    def from_x(size):
        return [(aligned(peer_x(d)[0], size), peer_x(d)[0]) for d in range(1, NX)]

    def start_all(copies):
        for copy in copies:
            copy.start()

    def wait_from(ref, semaphore, parts):
        for rows, place in parts:
            remote(ref.at[rows], ref.at[rows], semaphore.at[place], semaphore.at[place], sibling).wait_recv()

    def a_copies(k):
        if TYPES[k] == 0:
            plan = [(aligned(1 - along_y, M // 2), pl.ds(0, M // 2), 0, 0, across)]
        else:
            plan = to_x(k, 2 * MC)
        return [remote(qs.at[k, r], q1.at[k, t], a_send.at[k, i], a_recv.at[k, j], v) for r, t, i, j, v in plan]

    def project(k):
        x_copy(k).wait_recv()
        x = xs[k]
        g = jnp.dot(x, wg[...], preferred_element_type=F32)
        u = jnp.dot(x, wu[...], preferred_element_type=F32)
        encode(qs.at[k], [g, u])
        start_all(a_copies(k))

    def b_copies(k):
        if TYPES[k] == 0:
            plan = to_x(k, MC)
        else:
            plan = [(aligned(1 - along_y, MC), pl.ds(0, MC), 0, 0, across)]
        return [remote(qm.at[k, r], q2.at[k, t], b_send.at[k, i], b_recv.at[k, j], v) for r, t, i, j, v in plan]

    def pair(k):
        if TYPES[k] == 0:
            parts, own, size = [(pl.ds(0, M // 2), 0)], along_y, M // 2
        else:
            parts, own, size = from_x(2 * MC), along_x, 2 * MC
        wait_from(q1.at[k], a_recv.at[k], parts)
        total = decode(qs.at[k, aligned(own, size)])
        for rows, _ in parts:
            total = total + decode(q1.at[k, rows])
        encode(qm.at[k, pl.ds(0, size)], [total])
        start_all(b_copies(k))

    def block_of(k):
        return NX * along_y + along_x if TYPES[k] == 0 else 2 * along_x + along_y

    def h_copies(k):
        block = hid.at[k, aligned(block_of(k), MC), mine]
        if TYPES[k] == 0:
            plan = [(d, along_x, peer_x(d)[1]) for d in range(1, NX)]
        else:
            plan = [(0, 0, across)]
        return [remote(block, block, h_send.at[k, i], h_recv.at[k, j], v) for i, j, v in plan]

    def activate(k):
        if TYPES[k] == 0:
            parts, own = from_x(MC), along_x
        else:
            parts, own = [(pl.ds(0, MC), 0)], along_y
        wait_from(q2.at[k], b_recv.at[k], parts)
        total = decode(qm.at[k, aligned(own, MC)])
        for rows, _ in parts:
            total = total + decode(q2.at[k, rows])
        g, u = total[:, :half], total[:, half:]
        hid[k, aligned(block_of(k), MC), mine] = (g / (1.0 + jnp.exp(-g)) * u).astype(BF16)
        start_all(h_copies(k))

    def held(k):
        return aligned(along_y, M // 2) if TYPES[k] == 0 else aligned(along_x, 2 * MC)

    def g_copies(k):
        block = hid.at[k, held(k), mine]
        if TYPES[k] == 0:
            plan = [(0, 0, across)]
        else:
            plan = [(d, along_x, peer_x(d)[1]) for d in range(1, NX)]
        return [remote(block, block, g_send.at[k, i], g_recv.at[k, j], v) for i, j, v in plan]

    def g_parts(k):
        return [(aligned(1 - along_y, M // 2), 0)] if TYPES[k] == 0 else from_x(2 * MC)

    def f_copies(k):
        spots = [held(k)] + [rows for rows, _ in g_parts(k)]
        return [
            remote(hid.at[k, rows, mine], hid.at[k, rows, mine], f_send.at[k, i], f_recv.at[k, i], sibling)
            for i, rows in enumerate(spots)
        ]

    def spread(k):
        if TYPES[k] == 0:
            parts = [(aligned(NX * along_y + peer_x(d)[0], MC), peer_x(d)[0]) for d in range(1, NX)]
        else:
            parts = [(aligned(2 * along_x + 1 - along_y, MC), 0)]
        wait_from(hid.at[k, :, mine], h_recv.at[k], parts)
        start_all(g_copies(k))
        f_copies(k)[0].start()

    def forward(k):
        for part, copy in zip(g_parts(k), f_copies(k)[1:], strict=True):
            wait_from(hid.at[k, :, mine], g_recv.at[k], [part])
            copy.start()

    def owner(k, i):
        return CHIPS * (i % 2) + (i // 2 * 2 + k % 2 + 4 * (k // 2)) % CHIPS

    def owned(k):
        return (gy + 4 * (k // 2)) % CHIPS // 2 * 2 + gy // CHIPS

    def owns(k):
        return gy % 2 == k % 2

    def z_copy(k, i):
        rows = aligned(i, MZ)
        return remote(zs.at[k, rows], zr.at[k // 2, gy], z_send.at[k, i], z_recv.at[k // 2, gy], (gx, owner(k, i)))

    def contract(k):
        for copy in f_copies(k):
            copy.wait_recv()
        o = jnp.dot(hid[k], wd[...], preferred_element_type=F32)
        part[k] = o
        zs[k] = o.astype(BF16)

        def start_out(i, carry):
            @pl.when(owner(k, i) != gy)
            def _():
                z_copy(k, i).start()

            return carry

        lax.fori_loop(0, OWNERS, start_out, 0)

    def e_copy(k, i):
        block = OWNERS * k + owned(k)
        to = block // 4 + i
        place = block - 4 * to + 16
        return to, place, remote(ecode.at[k // 2], fin.at[place], e_send.at[k // 2, i], e_recv.at[place], (gx, to))

    def e_local_copy(k, place):
        return pltpu.make_async_copy(ecode.at[k // 2], fin.at[place], e_local.at[k // 2])

    def collect(k):
        @pl.when(owns(k))
        def _():
            zk = zr.at[k // 2]

            def add(d, total):
                source = (gy + d) % N
                remote(zk.at[source], zk.at[source], z_send.at[k, 0], z_recv.at[k // 2, source], sibling).wait_recv()
                return total + zk[source].astype(F32)

            total = lax.fori_loop(1, N, add, part[k, aligned(owned(k), MZ), :])
            encode(ecode.at[k // 2], [total])
            for i in range(DEST):
                to, place, copy = e_copy(k, i)

                @pl.when(to == gy)
                def _():
                    e_local_copy(k, place).start()

                @pl.when(to != gy)
                def _():
                    copy.start()

    def run(step, k):
        with jax.named_scope(f"{step.__name__}{k}"):
            step(k)

    steps = (project, pair, activate, spread, forward, contract, collect)
    for step, k in ORDER:
        if (step, k) == (5, 0):
            local[3].wait()
        run(steps[step], k)

    def wait_rows(place, carry):
        block = 4 * gy - 16 + place
        source = owner(block // OWNERS, block % OWNERS)

        @pl.when((block >= 0) & (block < LIVE // MZ) & (source != gy))
        def _():
            remote(ecode.at[0], fin.at[place], e_send.at[0, 0], e_recv.at[place], sibling).wait_recv()

        return carry

    with jax.named_scope("rows"):
        lax.fori_loop(0, WINDOW, wait_rows, 0)
    for k in range(CHUNKS):
        for i in range(DEST):
            to, place, copy = e_copy(k, i)

            @pl.when(owns(k) & (to == gy))
            def _():
                e_local_copy(k, place).wait()

    my_count, my_first = jnp.int32(0), jnp.int32(0)
    for g in range(N):
        my_count = my_count + jnp.where(g == gy, count[g], 0)
        my_first = my_first + jnp.where(g < gy, count[g], 0)
    slot = lax.broadcasted_iota(I32, (ROWS, WINDOW * MZ), 0)
    live = lax.broadcasted_iota(I32, (ROWS, WINDOW * MZ), 1) + (ROWS * gy - 256) - my_first
    pick = jnp.where((live == slot) & (slot < my_count), 1.0, 0.0).astype(BF16)
    rest = decode(fin).reshape(WINDOW * MZ, width)
    total = jnp.zeros((ROWS, width), F32)
    for _ in range(3):
        term = rest.astype(BF16)
        total = total + jnp.dot(pick, term, preferred_element_type=F32)
        rest = rest - term.astype(F32)
    out[...] = total

    for copy in weights:
        copy.wait_send()

    def sent_tokens(d, carry):
        token_copy(d).wait_send()
        return carry

    lax.fori_loop(1, N, sent_tokens, 0)
    for k in range(CHUNKS):
        for copy in [x_copy(k)] + a_copies(k) + b_copies(k) + h_copies(k) + g_copies(k) + f_copies(k):
            copy.wait_send()

        def sent_out(i, carry, k=k):
            @pl.when(owner(k, i) != gy)
            def _():
                z_copy(k, i).wait_send()

            return carry

        lax.fori_loop(0, OWNERS, sent_out, 0)
        for i in range(DEST):
            to, place, copy = e_copy(k, i)

            @pl.when(owns(k) & (to != gy))
            def _():
                copy.wait_send()


def body(tokens, gate, up, down, counts):
    depth, hidden = gate.shape
    width = down.shape[1]
    half = hidden // 2
    code = 2 * half + 128
    dma = pltpu.SemaphoreType.DMA
    any_space = pl.BlockSpec(memory_space=pl.ANY)
    return pl.pallas_call(
        kernel,
        out_shape=jax.ShapeDtypeStruct((ROWS, width), F32),
        in_specs=[pl.BlockSpec(memory_space=pltpu.SMEM)] + [any_space] * 4,
        out_specs=pl.BlockSpec(memory_space=pltpu.VMEM),
        scratch_shapes=[
            pltpu.VMEM((N * ROWS, depth), BF16),
            pltpu.VMEM((2 * depth, half), BF16),
            pltpu.VMEM((2 * depth, half), BF16),
            pltpu.VMEM((hidden, width), BF16),
            pltpu.VMEM((CHUNKS, M, 2 * depth), BF16),
            pltpu.VMEM((CHUNKS, M, code), I16),
            pltpu.VMEM((CHUNKS, M, code), I16),
            pltpu.VMEM((CHUNKS, M // 2, code), I16),
            pltpu.VMEM((CHUNKS, M // 2, code), I16),
            pltpu.VMEM((CHUNKS, M, hidden), BF16),
            pltpu.VMEM((CHUNKS, M, width), F32),
            pltpu.VMEM((CHUNKS, M, width), BF16),
            pltpu.VMEM((CHUNKS // 2, N, MZ, width), BF16),
            pltpu.VMEM((CHUNKS // 2, MZ, width + 128), I16),
            pltpu.VMEM((WINDOW, MZ, width + 128), I16),
            dma((4,)),
            dma((N,)), dma((N,)),
            dma((2,)), dma((2,)),
            dma((CHUNKS,)), dma((CHUNKS,)),
            dma((CHUNKS, NX)), dma((CHUNKS, NX)),
            dma((CHUNKS, NX)), dma((CHUNKS, NX)),
            dma((CHUNKS, NX)), dma((CHUNKS, NX)),
            dma((CHUNKS, NX)), dma((CHUNKS, NX)),
            dma((CHUNKS, NX)), dma((CHUNKS, NX)),
            dma((CHUNKS, OWNERS)), dma((CHUNKS // 2, N)),
            dma((CHUNKS // 2, DEST)), dma((WINDOW,)),
            dma((CHUNKS // 2,)),
        ],
        compiler_params=pltpu.CompilerParams(
            collective_id=0, has_side_effects=True, vmem_limit_bytes=56 * 2**20
        ),
        name="swiglu",
    )(counts, tokens, gate, up, down)


def solution(mesh):
    in_specs = (P("gx", None), P("gx", "gy"), P("gx", "gy"), P("gy", "gx"), P())
    out_specs = P("gy", "gx")
    return jax.shard_map(body, mesh=mesh, in_specs=in_specs, out_specs=out_specs, check_vma=False)
```

```python
import functools

import jax
import jax.numpy as jnp
from jax import lax
from jax.experimental import pallas as pl
from jax.experimental.pallas import tpu as pltpu
from jax.sharding import PartitionSpec as P

MESH = pl.DeviceIdType.MESH
BF16, F32, I16, I32 = jnp.bfloat16, jnp.float32, jnp.int16, jnp.int32

N = 16
CHIPS = 8
NX = 4
ROWS = 64
LIVE = 768
TYPES = (1, 1, 0, 0, 0, 0)
CHUNKS = len(TYPES)
M = LIVE // CHUNKS
MC = M // CHIPS
MZ = 16
OWNERS = M // MZ
ORDER = (
    (7, 3), (7, 0), (7, 1), (0, 3), (0, 1), (7, 2), (0, 2), (7, 5), (1, 3), (7, 4), (0, 0), (1, 1),
    (0, 4), (2, 1), (2, 3), (1, 2), (1, 0), (3, 1), (3, 3), (1, 4), (2, 0), (0, 5), (4, 3), (2, 2),
    (3, 0), (4, 1), (5, 3), (5, 1), (2, 4), (3, 2), (1, 5), (4, 0), (3, 4), (5, 0), (4, 2), (2, 5),
    (5, 2), (4, 4), (3, 5), (5, 4), (4, 5), (5, 5), (6, 3), (6, 0), (6, 2), (6, 4), (6, 1), (6, 5),
)
SPAN = 6
WINDOW = 20
DEST = 5
FULL = 32000.0


def mod(a, b):
    return a % b if isinstance(a, int) else lax.rem(a, jnp.int32(b))


def div(a, b):
    return a // b if isinstance(a, int) else lax.div(a, jnp.int32(b))


def aligned(index, unit):
    return pl.ds(pl.multiple_of(index * unit, unit), unit)


def kernel(
    counts, tokens, gate, up, down, out,
    tok, wg, wu, wd, xs, qs, q1, qm, q2, hid, part, zs, zr, ecode, fin,
    local_sem, tok_send, tok_recv, w_send, w_recv, x_send, x_recv,
    a_send, a_recv, b_send, b_recv, h_send, h_recv, g_send, g_recv, f_send, f_recv,
    z_send, z_recv, e_send, e_recv, e_local,
):
    gx, gy = lax.axis_index("gx"), lax.axis_index("gy")
    along_x, along_y, core = div(gx, 4), mod(div(gx, 2), 2), mod(gx, 2)
    depth = gate.shape[0]
    half = gate.shape[1] // 2
    width = down.shape[1]
    sibling = (gx + 1 - 2 * core, gy)
    across = (gx + 2 - 4 * along_y, gy)

    def remote(src, dst, send, recv, device):
        return pltpu.make_async_remote_copy(
            src_ref=src, dst_ref=dst, send_sem=send, recv_sem=recv, device_id=device, device_id_type=MESH
        )

    def peer_x(d):
        to = mod(along_x + d, NX)
        return to, (4 * to + 2 * along_y + core, gy)

    mine = aligned(core, half)
    my_rows = aligned(core, depth)
    local = [
        pltpu.make_async_copy(tokens.at[:, aligned(gx, depth)], tok.at[aligned(gx, ROWS)], local_sem.at[0]),
        pltpu.make_async_copy(gate.at[:, mine], wg.at[my_rows], local_sem.at[1]),
        pltpu.make_async_copy(up.at[:, mine], wu.at[my_rows], local_sem.at[2]),
        pltpu.make_async_copy(down, wd, local_sem.at[3]),
    ]
    for copy in local:
        copy.start()
    fin[...] = jnp.zeros_like(fin)

    barrier = pltpu.get_barrier_semaphore()

    def greet(d, carry):
        pl.semaphore_signal(barrier, inc=1, device_id=(mod(gx + d, N), gy), device_id_type=MESH)
        pl.semaphore_signal(barrier, inc=1, device_id=(gx, mod(gy + d, N)), device_id_type=MESH)
        return carry

    with jax.named_scope("enter"):
        lax.fori_loop(1, N, greet, 0)
        pl.semaphore_wait(barrier, 2 * (N - 1))

    def token_copy(d):
        to = mod(gx + d, N)
        return remote(
            tokens.at[:, aligned(to, depth)], tok.at[aligned(gx, ROWS)], tok_send.at[d], tok_recv.at[gx], (to, gy)
        )

    def start_tokens(d, carry):
        token_copy(d).start()
        return carry

    lax.fori_loop(1, N, start_tokens, 0)

    theirs = aligned(1 - core, half)
    weights = [
        remote(gate.at[:, theirs], wg.at[my_rows], w_send.at[0], w_recv.at[0], sibling),
        remote(up.at[:, theirs], wu.at[my_rows], w_send.at[1], w_recv.at[1], sibling),
    ]
    for copy in weights:
        copy.start()

    count = [counts[g] for g in range(N)]
    first = [jnp.int32(0)]
    for g in range(N - 1):
        first.append(first[-1] + count[g])

    def wait_tokens(g, carry):
        @pl.when(g != gx)
        def _():
            remote(tok.at[aligned(g, ROWS)], tok.at[aligned(g, ROWS)], tok_send.at[0], tok_recv.at[g], (g, gy)).wait_recv()

        return carry

    def compact(k):
        lane = lax.broadcasted_iota(I32, (1, SPAN * ROWS), 1)
        place = jnp.full((1, SPAN * ROWS), -1, I32)
        for i in range(SPAN):
            g = 2 * k + i
            slot = lane - ROWS * i
            place = jnp.where((slot >= 0) & (slot < count[g]), slot + (first[g] - M * k), place)
        row = lax.broadcasted_iota(I32, (M, SPAN * ROWS), 0)
        pick = jnp.where(row == place, 1.0, 0.0).astype(BF16)
        rows = jnp.dot(pick, tok[pl.ds(2 * k * ROWS, SPAN * ROWS), :], preferred_element_type=F32)
        xs[k, :, my_rows] = rows.astype(BF16)

    def x_copy(k):
        return remote(xs.at[k, :, my_rows], xs.at[k, :, my_rows], x_send.at[k], x_recv.at[k], sibling)

    local[0].wait()
    seen = set()

    def arrange(k):
        for g in range(2 * k, 2 * k + SPAN):
            if g not in seen:
                seen.add(g)
                wait_tokens(g, 0)
        compact(k)
        x_copy(k).start()

    def encode(ref, parts):
        top = functools.reduce(jnp.maximum, [jnp.max(jnp.abs(v), axis=1, keepdims=True) for v in parts])
        level = jnp.ceil(jnp.log(jnp.maximum(top, 1e-30)) * (64.0 / 0.6931471805599453)) + 1.0
        to_code = FULL * jnp.exp2(level * (-1.0 / 64.0))
        at = 0
        for v in parts:
            ref[:, at : at + v.shape[1]] = jnp.round(v * to_code).astype(I32).astype(I16)
            at += v.shape[1]
        ref[:, at:] = jnp.broadcast_to(level.astype(I32), (top.shape[0], 128)).astype(I16)

    def decode(ref):
        block = ref[...].astype(I32).astype(F32)
        used = block.shape[-1] - 128
        return block[..., :used] * (jnp.exp2(block[..., used : used + 1] * (1.0 / 64.0)) * (1.0 / FULL))

    def to_x(k, size, rows=None):
        copies = []
        for d in range(1, NX):
            to, device = peer_x(d)
            copies.append((aligned(to if rows is None else rows, size), aligned(along_x, size), d, along_x, device))
        return copies

    def from_x(size):
        return [(aligned(peer_x(d)[0], size), peer_x(d)[0]) for d in range(1, NX)]

    def start_all(copies):
        for copy in copies:
            copy.start()

    def wait_from(ref, semaphore, parts):
        for rows, place in parts:
            remote(ref.at[rows], ref.at[rows], semaphore.at[place], semaphore.at[place], sibling).wait_recv()

    def a_copies(k):
        if TYPES[k] == 0:
            plan = [(aligned(1 - along_y, M // 2), pl.ds(0, M // 2), 0, 0, across)]
        else:
            plan = to_x(k, 2 * MC)
        return [remote(qs.at[k, r], q1.at[k, t], a_send.at[k, i], a_recv.at[k, j], v) for r, t, i, j, v in plan]

    def project(k):
        x_copy(k).wait_recv()
        x = xs[k]
        g = jnp.dot(x, wg[...], preferred_element_type=F32)
        u = jnp.dot(x, wu[...], preferred_element_type=F32)
        encode(qs.at[k], [g, u])
        start_all(a_copies(k))

    def b_copies(k):
        if TYPES[k] == 0:
            plan = to_x(k, MC)
        else:
            plan = [(aligned(1 - along_y, MC), pl.ds(0, MC), 0, 0, across)]
        return [remote(qm.at[k, r], q2.at[k, t], b_send.at[k, i], b_recv.at[k, j], v) for r, t, i, j, v in plan]

    def pair(k):
        if TYPES[k] == 0:
            parts, own, size = [(pl.ds(0, M // 2), 0)], along_y, M // 2
        else:
            parts, own, size = from_x(2 * MC), along_x, 2 * MC
        wait_from(q1.at[k], a_recv.at[k], parts)
        total = decode(qs.at[k, aligned(own, size)])
        for rows, _ in parts:
            total = total + decode(q1.at[k, rows])
        encode(qm.at[k, pl.ds(0, size)], [total])
        start_all(b_copies(k))

    def block_of(k):
        return NX * along_y + along_x if TYPES[k] == 0 else 2 * along_x + along_y

    def h_copies(k):
        block = hid.at[k, aligned(block_of(k), MC), mine]
        if TYPES[k] == 0:
            plan = [(d, along_x, peer_x(d)[1]) for d in range(1, NX)]
        else:
            plan = [(0, 0, across)]
        return [remote(block, block, h_send.at[k, i], h_recv.at[k, j], v) for i, j, v in plan]

    def activate(k):
        if TYPES[k] == 0:
            parts, own = from_x(MC), along_x
        else:
            parts, own = [(pl.ds(0, MC), 0)], along_y
        wait_from(q2.at[k], b_recv.at[k], parts)
        total = decode(qm.at[k, aligned(own, MC)])
        for rows, _ in parts:
            total = total + decode(q2.at[k, rows])
        g, u = total[:, :half], total[:, half:]
        hid[k, aligned(block_of(k), MC), mine] = (g / (1.0 + jnp.exp(-g)) * u).astype(BF16)
        start_all(h_copies(k))

    def held(k):
        return aligned(along_y, M // 2) if TYPES[k] == 0 else aligned(along_x, 2 * MC)

    def g_copies(k):
        block = hid.at[k, held(k), mine]
        if TYPES[k] == 0:
            plan = [(0, 0, across)]
        else:
            plan = [(d, along_x, peer_x(d)[1]) for d in range(1, NX)]
        return [remote(block, block, g_send.at[k, i], g_recv.at[k, j], v) for i, j, v in plan]

    def g_parts(k):
        return [(aligned(1 - along_y, M // 2), 0)] if TYPES[k] == 0 else from_x(2 * MC)

    def f_copies(k):
        spots = [held(k)] + [rows for rows, _ in g_parts(k)]
        return [
            remote(hid.at[k, rows, mine], hid.at[k, rows, mine], f_send.at[k, i], f_recv.at[k, i], sibling)
            for i, rows in enumerate(spots)
        ]

    def spread(k):
        if TYPES[k] == 0:
            parts = [(aligned(NX * along_y + peer_x(d)[0], MC), peer_x(d)[0]) for d in range(1, NX)]
        else:
            parts = [(aligned(2 * along_x + 1 - along_y, MC), 0)]
        wait_from(hid.at[k, :, mine], h_recv.at[k], parts)
        start_all(g_copies(k))
        f_copies(k)[0].start()

    def forward(k):
        for part, copy in zip(g_parts(k), f_copies(k)[1:], strict=True):
            wait_from(hid.at[k, :, mine], g_recv.at[k], [part])
            copy.start()

    def owner(k, i):
        return CHIPS * mod(i, 2) + mod(div(i, 2) * 2 + mod(k, 2) + 4 * div(k, 2), CHIPS)

    def owned(k):
        return div(mod(gy + 4 * (k // 2), CHIPS), 2) * 2 + div(gy, CHIPS)

    def owns(k):
        return mod(gy, 2) == k % 2

    def z_copy(k, i):
        rows = aligned(i, MZ)
        return remote(zs.at[k, rows], zr.at[k // 2, gy], z_send.at[k, i], z_recv.at[k // 2, gy], (gx, owner(k, i)))

    def contract(k):
        for copy in f_copies(k):
            copy.wait_recv()
        o = jnp.dot(hid[k], wd[...], preferred_element_type=F32)
        part[k] = o
        zs[k] = o.astype(BF16)

        def start_out(j, carry):
            z_copy(k, mod(owned(k) + j, OWNERS)).start()
            return carry

        lax.fori_loop(jnp.where(owns(k), 1, 0), OWNERS, start_out, 0)

    def e_copy(k, i):
        block = OWNERS * k + owned(k)
        to = div(block, 4) + i
        place = block - 4 * to + 16
        return to, place, remote(ecode.at[k // 2], fin.at[place], e_send.at[k // 2, i], e_recv.at[place], (gx, to))

    def e_local_copy(k, place):
        return pltpu.make_async_copy(ecode.at[k // 2], fin.at[place], e_local.at[k // 2])

    def collect(k):
        @pl.when(owns(k))
        def _():
            zk = zr.at[k // 2]

            def add(d, total):
                source = mod(gy + d, N)
                remote(zk.at[source], zk.at[source], z_send.at[k, 0], z_recv.at[k // 2, source], sibling).wait_recv()
                return total + zk[source].astype(F32)

            total = lax.fori_loop(1, N, add, part[k, aligned(owned(k), MZ), :])
            encode(ecode.at[k // 2], [total])
            for i in range(DEST):
                to, place, copy = e_copy(k, i)

                @pl.when(to == gy)
                def _():
                    e_local_copy(k, place).start()

                @pl.when(to != gy)
                def _():
                    copy.start()

    steps = (project, pair, activate, spread, forward, contract, collect, arrange)
    for step, k in ORDER:
        if (step, k) == (0, 3):
            for copy in local[1:3]:
                copy.wait()
            for copy in weights:
                copy.wait_recv()
        if (step, k) == (5, 3):
            local[3].wait()
        steps[step](k)

    def wait_rows(place, carry):
        block = 4 * gy - 16 + place
        at = jnp.maximum(block, 0)
        source = owner(div(at, OWNERS), mod(at, OWNERS))

        @pl.when((block >= 0) & (block < LIVE // MZ) & (source != gy))
        def _():
            remote(ecode.at[0], fin.at[place], e_send.at[0, 0], e_recv.at[place], sibling).wait_recv()

        return carry

    with jax.named_scope("rows"):
        lax.fori_loop(0, WINDOW, wait_rows, 0)
    for k in range(CHUNKS):
        for i in range(DEST):
            to, place, copy = e_copy(k, i)

            @pl.when(owns(k) & (to == gy))
            def _():
                e_local_copy(k, place).wait()

    my_count, my_first = jnp.int32(0), jnp.int32(0)
    for g in range(N):
        my_count = my_count + jnp.where(g == gy, count[g], 0)
        my_first = my_first + jnp.where(g < gy, count[g], 0)
    slot = lax.broadcasted_iota(I32, (ROWS, WINDOW * MZ), 0)
    live = lax.broadcasted_iota(I32, (ROWS, WINDOW * MZ), 1) + (ROWS * gy - 256) - my_first
    pick = jnp.where((live == slot) & (slot < my_count), 1.0, 0.0).astype(BF16)
    rest = decode(fin).reshape(WINDOW * MZ, width)
    total = jnp.zeros((ROWS, width), F32)
    for _ in range(3):
        term = rest.astype(BF16)
        total = total + jnp.dot(pick, term, preferred_element_type=F32)
        rest = rest - term.astype(F32)
    out[...] = total

    for copy in weights:
        copy.wait_send()

    def sent_tokens(d, carry):
        token_copy(d).wait_send()
        return carry

    lax.fori_loop(1, N, sent_tokens, 0)
    for k in range(CHUNKS):
        for copy in [x_copy(k)] + a_copies(k) + b_copies(k) + h_copies(k) + g_copies(k) + f_copies(k):
            copy.wait_send()

        def sent_out(j, carry, k=k):
            z_copy(k, mod(owned(k) + j, OWNERS)).wait_send()
            return carry

        lax.fori_loop(jnp.where(owns(k), 1, 0), OWNERS, sent_out, 0)
        for i in range(DEST):
            to, place, copy = e_copy(k, i)

            @pl.when(owns(k) & (to != gy))
            def _():
                copy.wait_send()


def body(tokens, gate, up, down, counts):
    depth, hidden = gate.shape
    width = down.shape[1]
    half = hidden // 2
    code = 2 * half + 128
    dma = pltpu.SemaphoreType.DMA
    any_space = pl.BlockSpec(memory_space=pl.ANY)
    return pl.pallas_call(
        kernel,
        out_shape=jax.ShapeDtypeStruct((ROWS, width), F32),
        in_specs=[pl.BlockSpec(memory_space=pltpu.SMEM)] + [any_space] * 4,
        out_specs=pl.BlockSpec(memory_space=pltpu.VMEM),
        scratch_shapes=[
            pltpu.VMEM((N * ROWS, depth), BF16),
            pltpu.VMEM((2 * depth, half), BF16),
            pltpu.VMEM((2 * depth, half), BF16),
            pltpu.VMEM((hidden, width), BF16),
            pltpu.VMEM((CHUNKS, M, 2 * depth), BF16),
            pltpu.VMEM((CHUNKS, M, code), I16),
            pltpu.VMEM((CHUNKS, M, code), I16),
            pltpu.VMEM((CHUNKS, M // 2, code), I16),
            pltpu.VMEM((CHUNKS, M // 2, code), I16),
            pltpu.VMEM((CHUNKS, M, hidden), BF16),
            pltpu.VMEM((CHUNKS, M, width), F32),
            pltpu.VMEM((CHUNKS, M, width), BF16),
            pltpu.VMEM((CHUNKS // 2, N, MZ, width), BF16),
            pltpu.VMEM((CHUNKS // 2, MZ, width + 128), I16),
            pltpu.VMEM((WINDOW, MZ, width + 128), I16),
            dma((4,)),
            dma((N,)), dma((N,)),
            dma((2,)), dma((2,)),
            dma((CHUNKS,)), dma((CHUNKS,)),
            dma((CHUNKS, NX)), dma((CHUNKS, NX)),
            dma((CHUNKS, NX)), dma((CHUNKS, NX)),
            dma((CHUNKS, NX)), dma((CHUNKS, NX)),
            dma((CHUNKS, NX)), dma((CHUNKS, NX)),
            dma((CHUNKS, NX)), dma((CHUNKS, NX)),
            dma((CHUNKS, OWNERS)), dma((CHUNKS // 2, N)),
            dma((CHUNKS // 2, DEST)), dma((WINDOW,)),
            dma((CHUNKS // 2,)),
        ],
        compiler_params=pltpu.CompilerParams(
            collective_id=0, has_side_effects=True, vmem_limit_bytes=56 * 2**20
        ),
        name="swiglu",
    )(counts, tokens, gate, up, down)


def solution(mesh):
    in_specs = (P("gx", None), P("gx", "gy"), P("gx", "gy"), P("gy", "gx"), P())
    out_specs = P("gy", "gx")
    return jax.shard_map(body, mesh=mesh, in_specs=in_specs, out_specs=out_specs, check_vma=False)
```

```python
import functools

import jax
import jax.numpy as jnp
from jax import lax
from jax.experimental import pallas as pl
from jax.experimental.pallas import tpu as pltpu
from jax.sharding import PartitionSpec as P

MESH = pl.DeviceIdType.MESH
BF16, F32, I16, I32 = jnp.bfloat16, jnp.float32, jnp.int16, jnp.int32

N = 16
CHIPS = 8
NX = 4
ROWS = 64
LIVE = 768
TYPES = (1, 0, 1, 0, 0, 0)
CHUNKS = len(TYPES)
M = LIVE // CHUNKS
MC = M // CHIPS
MZ = 16
OWNERS = M // MZ
ORDER = (
    (7, 1), (7, 3), (7, 4), (7, 2), (0, 1), (0, 3), (0, 2), (7, 0), (1, 1), (7, 5), (0, 0), (1, 2),
    (0, 5), (2, 1), (1, 3), (2, 2), (1, 0), (1, 5), (3, 1), (3, 2), (2, 0), (0, 4), (4, 1), (2, 5),
    (3, 0), (5, 1), (2, 3), (4, 2), (3, 5), (5, 2), (1, 4), (4, 0), (5, 0), (3, 3), (4, 5), (2, 4),
    (5, 5), (4, 3), (3, 4), (5, 3), (4, 4), (6, 2), (6, 1), (5, 4), (6, 5), (6, 3), (6, 0), (6, 4),
)
SPAN = 6
WINDOW = 20
DEST = 5
FULL = 32000.0


def mod(a, b):
    return a % b if isinstance(a, int) else lax.rem(a, jnp.int32(b))


def div(a, b):
    return a // b if isinstance(a, int) else lax.div(a, jnp.int32(b))


def aligned(index, unit):
    return pl.ds(pl.multiple_of(index * unit, unit), unit)


def kernel(
    counts, tokens, gate, up, down, out,
    tok, wg, wu, wd, xs, qs, q1, qm, q2, hid, part, zs, zr, ecode, fin,
    local_sem, tok_send, tok_recv, w_send, w_recv, x_send, x_recv,
    a_send, a_recv, b_send, b_recv, h_send, h_recv, g_send, g_recv, f_send, f_recv,
    z_send, z_recv, e_send, e_recv, e_local,
):
    gx, gy = lax.axis_index("gx"), lax.axis_index("gy")
    along_x, along_y, core = div(gx, 4), mod(div(gx, 2), 2), mod(gx, 2)
    depth = gate.shape[0]
    half = gate.shape[1] // 2
    width = down.shape[1]
    sibling = (gx + 1 - 2 * core, gy)
    across = (gx + 2 - 4 * along_y, gy)

    def remote(src, dst, send, recv, device):
        return pltpu.make_async_remote_copy(
            src_ref=src, dst_ref=dst, send_sem=send, recv_sem=recv, device_id=device, device_id_type=MESH
        )

    def peer_x(d):
        to = mod(along_x + d, NX)
        return to, (4 * to + 2 * along_y + core, gy)

    mine = aligned(core, half)
    my_rows = aligned(core, depth)
    local = [
        pltpu.make_async_copy(tokens.at[:, aligned(gx, depth)], tok.at[aligned(gx, ROWS)], local_sem.at[0]),
        pltpu.make_async_copy(gate.at[:, mine], wg.at[my_rows], local_sem.at[1]),
        pltpu.make_async_copy(up.at[:, mine], wu.at[my_rows], local_sem.at[2]),
        pltpu.make_async_copy(down, wd, local_sem.at[3]),
    ]
    for copy in local:
        copy.start()
    fin[...] = jnp.zeros_like(fin)

    barrier = pltpu.get_barrier_semaphore()

    def greet(d, carry):
        pl.semaphore_signal(barrier, inc=1, device_id=(mod(gx + d, N), gy), device_id_type=MESH)
        pl.semaphore_signal(barrier, inc=1, device_id=(gx, mod(gy + d, N)), device_id_type=MESH)
        return carry

    with jax.named_scope("enter"):
        lax.fori_loop(1, N, greet, 0)
        pl.semaphore_wait(barrier, 2 * (N - 1))

    def token_copy(d):
        to = mod(gx + d, N)
        return remote(
            tokens.at[:, aligned(to, depth)], tok.at[aligned(gx, ROWS)], tok_send.at[d], tok_recv.at[gx], (to, gy)
        )

    def start_tokens(d, carry):
        token_copy(d).start()
        return carry

    lax.fori_loop(1, N, start_tokens, 0)

    theirs = aligned(1 - core, half)
    weights = [
        remote(gate.at[:, theirs], wg.at[my_rows], w_send.at[0], w_recv.at[0], sibling),
        remote(up.at[:, theirs], wu.at[my_rows], w_send.at[1], w_recv.at[1], sibling),
    ]
    for copy in weights:
        copy.start()

    count = [counts[g] for g in range(N)]
    first = [jnp.int32(0)]
    for g in range(N - 1):
        first.append(first[-1] + count[g])

    def wait_tokens(g, carry):
        @pl.when(g != gx)
        def _():
            remote(tok.at[aligned(g, ROWS)], tok.at[aligned(g, ROWS)], tok_send.at[0], tok_recv.at[g], (g, gy)).wait_recv()

        return carry

    def compact(k):
        lane = lax.broadcasted_iota(I32, (1, SPAN * ROWS), 1)
        place = jnp.full((1, SPAN * ROWS), -1, I32)
        for i in range(SPAN):
            g = 2 * k + i
            slot = lane - ROWS * i
            place = jnp.where((slot >= 0) & (slot < count[g]), slot + (first[g] - M * k), place)
        row = lax.broadcasted_iota(I32, (M, SPAN * ROWS), 0)
        pick = jnp.where(row == place, 1.0, 0.0).astype(BF16)
        rows = jnp.dot(pick, tok[pl.ds(2 * k * ROWS, SPAN * ROWS), :], preferred_element_type=F32)
        xs[k, :, my_rows] = rows.astype(BF16)

    def x_copy(k):
        return remote(xs.at[k, :, my_rows], xs.at[k, :, my_rows], x_send.at[k], x_recv.at[k], sibling)

    local[0].wait()
    seen = set()

    def arrange(k):
        for g in range(2 * k, 2 * k + SPAN):
            if g not in seen:
                seen.add(g)
                wait_tokens(g, 0)
        compact(k)
        x_copy(k).start()

    def encode(ref, parts):
        top = functools.reduce(jnp.maximum, [jnp.max(jnp.abs(v), axis=1, keepdims=True) for v in parts])
        level = jnp.ceil(jnp.log(jnp.maximum(top, 1e-30)) * (64.0 / 0.6931471805599453)) + 1.0
        to_code = FULL * jnp.exp2(level * (-1.0 / 64.0))
        at = 0
        for v in parts:
            ref[:, at : at + v.shape[1]] = jnp.round(v * to_code).astype(I32).astype(I16)
            at += v.shape[1]
        ref[:, at:] = jnp.broadcast_to(level.astype(I32), (top.shape[0], 128)).astype(I16)

    def decode(ref):
        block = ref[...].astype(I32).astype(F32)
        used = block.shape[-1] - 128
        return block[..., :used] * (jnp.exp2(block[..., used : used + 1] * (1.0 / 64.0)) * (1.0 / FULL))

    def to_x(k, size, rows=None):
        copies = []
        for d in range(1, NX):
            to, device = peer_x(d)
            copies.append((aligned(to if rows is None else rows, size), aligned(along_x, size), d, along_x, device))
        return copies

    def from_x(size):
        return [(aligned(peer_x(d)[0], size), peer_x(d)[0]) for d in range(1, NX)]

    def start_all(copies):
        for copy in copies:
            copy.start()

    def wait_from(ref, semaphore, parts):
        for rows, place in parts:
            remote(ref.at[rows], ref.at[rows], semaphore.at[place], semaphore.at[place], sibling).wait_recv()

    def a_copies(k):
        if TYPES[k] == 0:
            plan = [(aligned(1 - along_y, M // 2), pl.ds(0, M // 2), 0, 0, across)]
        else:
            plan = to_x(k, 2 * MC)
        return [remote(qs.at[k, r], q1.at[k, t], a_send.at[k, i], a_recv.at[k, j], v) for r, t, i, j, v in plan]

    def project(k):
        x_copy(k).wait_recv()
        x = xs[k]
        g = jnp.dot(x, wg[...], preferred_element_type=F32)
        u = jnp.dot(x, wu[...], preferred_element_type=F32)
        encode(qs.at[k], [g, u])
        start_all(a_copies(k))

    def b_copies(k):
        if TYPES[k] == 0:
            plan = to_x(k, MC)
        else:
            plan = [(aligned(1 - along_y, MC), pl.ds(0, MC), 0, 0, across)]
        return [remote(qm.at[k, r], q2.at[k, t], b_send.at[k, i], b_recv.at[k, j], v) for r, t, i, j, v in plan]

    def pair(k):
        if TYPES[k] == 0:
            parts, own, size = [(pl.ds(0, M // 2), 0)], along_y, M // 2
        else:
            parts, own, size = from_x(2 * MC), along_x, 2 * MC
        wait_from(q1.at[k], a_recv.at[k], parts)
        total = decode(qs.at[k, aligned(own, size)])
        for rows, _ in parts:
            total = total + decode(q1.at[k, rows])
        encode(qm.at[k, pl.ds(0, size)], [total])
        start_all(b_copies(k))

    def block_of(k):
        return NX * along_y + along_x if TYPES[k] == 0 else 2 * along_x + along_y

    def h_copies(k):
        block = hid.at[k, aligned(block_of(k), MC), mine]
        if TYPES[k] == 0:
            plan = [(d, along_x, peer_x(d)[1]) for d in range(1, NX)]
        else:
            plan = [(0, 0, across)]
        return [remote(block, block, h_send.at[k, i], h_recv.at[k, j], v) for i, j, v in plan]

    def activate(k):
        if TYPES[k] == 0:
            parts, own = from_x(MC), along_x
        else:
            parts, own = [(pl.ds(0, MC), 0)], along_y
        wait_from(q2.at[k], b_recv.at[k], parts)
        total = decode(qm.at[k, aligned(own, MC)])
        for rows, _ in parts:
            total = total + decode(q2.at[k, rows])
        g, u = total[:, :half], total[:, half:]
        hid[k, aligned(block_of(k), MC), mine] = (g / (1.0 + jnp.exp(-g)) * u).astype(BF16)
        start_all(h_copies(k))

    def held(k):
        return aligned(along_y, M // 2) if TYPES[k] == 0 else aligned(along_x, 2 * MC)

    def g_copies(k):
        block = hid.at[k, held(k), mine]
        if TYPES[k] == 0:
            plan = [(0, 0, across)]
        else:
            plan = [(d, along_x, peer_x(d)[1]) for d in range(1, NX)]
        return [remote(block, block, g_send.at[k, i], g_recv.at[k, j], v) for i, j, v in plan]

    def g_parts(k):
        return [(aligned(1 - along_y, M // 2), 0)] if TYPES[k] == 0 else from_x(2 * MC)

    def f_copies(k):
        spots = [held(k)] + [rows for rows, _ in g_parts(k)]
        return [
            remote(hid.at[k, rows, mine], hid.at[k, rows, mine], f_send.at[k, i], f_recv.at[k, i], sibling)
            for i, rows in enumerate(spots)
        ]

    def spread(k):
        if TYPES[k] == 0:
            parts = [(aligned(NX * along_y + peer_x(d)[0], MC), peer_x(d)[0]) for d in range(1, NX)]
        else:
            parts = [(aligned(2 * along_x + 1 - along_y, MC), 0)]
        wait_from(hid.at[k, :, mine], h_recv.at[k], parts)
        start_all(g_copies(k))
        f_copies(k)[0].start()

    def forward(k):
        for part, copy in zip(g_parts(k), f_copies(k)[1:], strict=True):
            wait_from(hid.at[k, :, mine], g_recv.at[k], [part])
            copy.start()

    def owner(k, i):
        return CHIPS * mod(i, 2) + mod(div(i, 2) * 2 + mod(k, 2) + 4 * div(k, 2), CHIPS)

    def owned(k):
        return div(mod(gy + 4 * (k // 2), CHIPS), 2) * 2 + div(gy, CHIPS)

    def owns(k):
        return mod(gy, 2) == k % 2

    def z_copy(k, i):
        rows = aligned(i, MZ)
        return remote(zs.at[k, rows], zr.at[k // 2, gy], z_send.at[k, i], z_recv.at[k // 2, gy], (gx, owner(k, i)))

    def contract(k):
        for copy in f_copies(k):
            copy.wait_recv()
        o = jnp.dot(hid[k], wd[...], preferred_element_type=F32)
        part[k] = o
        zs[k] = o.astype(BF16)

        def start_out(j, carry):
            z_copy(k, mod(owned(k) + j, OWNERS)).start()
            return carry

        lax.fori_loop(jnp.where(owns(k), 1, 0), OWNERS, start_out, 0)

    def e_copy(k, i):
        block = OWNERS * k + owned(k)
        to = div(block, 4) + i
        place = block - 4 * to + 16
        return to, place, remote(ecode.at[k // 2], fin.at[place], e_send.at[k // 2, i], e_recv.at[place], (gx, to))

    def e_local_copy(k, place):
        return pltpu.make_async_copy(ecode.at[k // 2], fin.at[place], e_local.at[k // 2])

    def collect(k):
        @pl.when(owns(k))
        def _():
            zk = zr.at[k // 2]

            def add(d, total):
                source = mod(gy + d, N)
                remote(zk.at[source], zk.at[source], z_send.at[k, 0], z_recv.at[k // 2, source], sibling).wait_recv()
                return total + zk[source].astype(F32)

            total = lax.fori_loop(1, N, add, part[k, aligned(owned(k), MZ), :])
            encode(ecode.at[k // 2], [total])
            for i in range(DEST):
                to, place, copy = e_copy(k, i)

                @pl.when(to == gy)
                def _():
                    e_local_copy(k, place).start()

                @pl.when(to != gy)
                def _():
                    copy.start()

    steps = (project, pair, activate, spread, forward, contract, collect, arrange)
    for step, k in ORDER:
        if (step, k) == (0, 1):
            for copy in local[1:3]:
                copy.wait()
            for copy in weights:
                copy.wait_recv()
        if (step, k) == (5, 1):
            local[3].wait()
        steps[step](k)

    def wait_rows(place, carry):
        block = 4 * gy - 16 + place
        at = jnp.maximum(block, 0)
        source = owner(div(at, OWNERS), mod(at, OWNERS))

        @pl.when((block >= 0) & (block < LIVE // MZ) & (source != gy))
        def _():
            remote(ecode.at[0], fin.at[place], e_send.at[0, 0], e_recv.at[place], sibling).wait_recv()

        return carry

    with jax.named_scope("rows"):
        lax.fori_loop(0, WINDOW, wait_rows, 0)
    for k in range(CHUNKS):
        for i in range(DEST):
            to, place, copy = e_copy(k, i)

            @pl.when(owns(k) & (to == gy))
            def _():
                e_local_copy(k, place).wait()

    my_count, my_first = jnp.int32(0), jnp.int32(0)
    for g in range(N):
        my_count = my_count + jnp.where(g == gy, count[g], 0)
        my_first = my_first + jnp.where(g < gy, count[g], 0)
    slot = lax.broadcasted_iota(I32, (ROWS, WINDOW * MZ), 0)
    live = lax.broadcasted_iota(I32, (ROWS, WINDOW * MZ), 1) + (ROWS * gy - 256) - my_first
    pick = jnp.where((live == slot) & (slot < my_count), 1.0, 0.0).astype(BF16)
    rest = decode(fin).reshape(WINDOW * MZ, width)
    total = jnp.zeros((ROWS, width), F32)
    for _ in range(3):
        term = rest.astype(BF16)
        total = total + jnp.dot(pick, term, preferred_element_type=F32)
        rest = rest - term.astype(F32)
    out[...] = total

    for copy in weights:
        copy.wait_send()

    def sent_tokens(d, carry):
        token_copy(d).wait_send()
        return carry

    lax.fori_loop(1, N, sent_tokens, 0)
    for k in range(CHUNKS):
        for copy in [x_copy(k)] + a_copies(k) + b_copies(k) + h_copies(k) + g_copies(k) + f_copies(k):
            copy.wait_send()

        def sent_out(j, carry, k=k):
            z_copy(k, mod(owned(k) + j, OWNERS)).wait_send()
            return carry

        lax.fori_loop(jnp.where(owns(k), 1, 0), OWNERS, sent_out, 0)
        for i in range(DEST):
            to, place, copy = e_copy(k, i)

            @pl.when(owns(k) & (to != gy))
            def _():
                copy.wait_send()


def body(tokens, gate, up, down, counts):
    depth, hidden = gate.shape
    width = down.shape[1]
    half = hidden // 2
    code = 2 * half + 128
    dma = pltpu.SemaphoreType.DMA
    any_space = pl.BlockSpec(memory_space=pl.ANY)
    return pl.pallas_call(
        kernel,
        out_shape=jax.ShapeDtypeStruct((ROWS, width), F32),
        in_specs=[pl.BlockSpec(memory_space=pltpu.SMEM)] + [any_space] * 4,
        out_specs=pl.BlockSpec(memory_space=pltpu.VMEM),
        scratch_shapes=[
            pltpu.VMEM((N * ROWS, depth), BF16),
            pltpu.VMEM((2 * depth, half), BF16),
            pltpu.VMEM((2 * depth, half), BF16),
            pltpu.VMEM((hidden, width), BF16),
            pltpu.VMEM((CHUNKS, M, 2 * depth), BF16),
            pltpu.VMEM((CHUNKS, M, code), I16),
            pltpu.VMEM((CHUNKS, M, code), I16),
            pltpu.VMEM((CHUNKS, M // 2, code), I16),
            pltpu.VMEM((CHUNKS, M // 2, code), I16),
            pltpu.VMEM((CHUNKS, M, hidden), BF16),
            pltpu.VMEM((CHUNKS, M, width), F32),
            pltpu.VMEM((CHUNKS, M, width), BF16),
            pltpu.VMEM((CHUNKS // 2, N, MZ, width), BF16),
            pltpu.VMEM((CHUNKS // 2, MZ, width + 128), I16),
            pltpu.VMEM((WINDOW, MZ, width + 128), I16),
            dma((4,)),
            dma((N,)), dma((N,)),
            dma((2,)), dma((2,)),
            dma((CHUNKS,)), dma((CHUNKS,)),
            dma((CHUNKS, NX)), dma((CHUNKS, NX)),
            dma((CHUNKS, NX)), dma((CHUNKS, NX)),
            dma((CHUNKS, NX)), dma((CHUNKS, NX)),
            dma((CHUNKS, NX)), dma((CHUNKS, NX)),
            dma((CHUNKS, NX)), dma((CHUNKS, NX)),
            dma((CHUNKS, OWNERS)), dma((CHUNKS // 2, N)),
            dma((CHUNKS // 2, DEST)), dma((WINDOW,)),
            dma((CHUNKS // 2,)),
        ],
        compiler_params=pltpu.CompilerParams(
            collective_id=0, has_side_effects=True, vmem_limit_bytes=56 * 2**20
        ),
        name="swiglu",
    )(counts, tokens, gate, up, down)


def solution(mesh):
    in_specs = (P("gx", None), P("gx", "gy"), P("gx", "gy"), P("gy", "gx"), P())
    out_specs = P("gy", "gx")
    return jax.shard_map(body, mesh=mesh, in_specs=in_specs, out_specs=out_specs, check_vma=False)
```
